32 devices in a mesh: section: 4 (over y, x), fsdp: 8 (over z, core).
Axes of the slice: x: 2, y: 2, z: 4, core: 2. Of those that a mesh axis runs over, the one named last changes fastest.
Arguments:
- inputs: bfloat16 [8, 128, 8192], P(None, 'fsdp'), may hold values from -6 to 6
- cotangent: bfloat16 [8, 128, 8192], P(None, 'fsdp'), may hold values from -6 to 6
- kv_weight: bfloat16 [4, 8192, 1024], P('section', 'fsdp'), may hold values from -0.0625 to 0.0625
- norm_gain: bfloat16 [4, 8192], P('section', 'fsdp'), may hold values from 0.25 to 1.75
Outputs:
- kv_grad: float32 [4, 8192, 1024], P('section', 'fsdp')
- gain_grad: float32 [4, 8192], P('section', 'fsdp')
The draws below stay inside these ranges and needn't reach their ends.
All inputs are finite; a program needn't handle non-finite values.
Results may differ from the reference program's by a relative error of at most 0.02.
Values may be sent and summed in bfloat16 or wider, within the bound.
A program may use at most 128 MiB of HBM per device.

```python
from functools import partial
import jax
import jax.numpy as jnp
from jax import lax

D = 8192
HD = 128
KVH = 4
SEQ = 16
MICRO = 8
SECTIONS = 4
TOKENS = 128
N_FSDP = 8


def block_levels(rng, dims, pieces, least, high):
    def one(axis_at, blocks):
        draws = jax.random.uniform(jax.random.fold_in(jax.random.fold_in(rng, 6), axis_at), (blocks,), jnp.float32, least / len(pieces), high / len(pieces))
        return jnp.repeat(jnp.exp(draws), dims[axis_at] // blocks).reshape((-1,) + (1,) * (len(dims) - axis_at - 1))

    factor_of = one(*pieces[0])
    for cut in pieces[1:]:
        factor_of = factor_of * one(*cut)
    return factor_of


def scatter_about(own_key, extent, deviation, bound, split=(), dtype=jnp.bfloat16):
    values = deviation * jax.random.normal(own_key, extent, jnp.float32)
    if split:
        values = values * block_levels(own_key, extent, split, -0.22, 0.18)
    return jnp.clip(values, -bound, bound).astype(dtype)


def setup_inputs(seed: int = 0) -> dict:
    key_list = jax.random.split(jax.random.key(seed), 5)
    inputs = scatter_about(key_list[0], (MICRO, TOKENS, D), 1.0, 6.0, ((1, 8),))
    cotangent = scatter_about(key_list[1], (MICRO, TOKENS, D), 1.0, 6.0, ((1, 8),))
    kv_weight = scatter_about(key_list[2], (SECTIONS, D, 2 * KVH * HD), D ** -0.5, 0.0625, ((0, 4), (1, 8)))
    norm_gain = jnp.clip(1.0 + 0.15 * jax.random.normal(key_list[3], (SECTIONS, D), jnp.float32), 0.25, 1.75).astype(jnp.bfloat16)
    return {"inputs": inputs, "cotangent": cotangent, "kv_weight": kv_weight, "norm_gain": norm_gain}


epsilon = 1e-05

def normalize(rows_f32, gain_f32):
    mean_sq = lax.optimization_barrier(jnp.mean(rows_f32 * rows_f32, axis=-1, keepdims=True))
    return rows_f32 * lax.rsqrt(mean_sq + epsilon) * gain_f32

def attend(normed, keyval, kv_heads, head_size):
    batch_size, length, model_width = normed.shape
    group = model_width // head_size // kv_heads
    kv_width = kv_heads * head_size
    queries = normed.reshape(batch_size, length, kv_heads, group, head_size).astype(jnp.float32)
    keys = keyval[:, :, :kv_width].reshape(batch_size, length, kv_heads, head_size).astype(jnp.float32)
    values = keyval[:, :, kv_width:].reshape(batch_size, length, kv_heads, head_size).astype(jnp.float32)
    scores = jnp.einsum('blkgd,bmkd->bkglm', queries, keys) * head_size ** (-0.5)
    position = jnp.arange(length)
    causal_mask = position[:, None] >= position[None, :]
    scores = jnp.where(causal_mask, scores, -1e+30)
    largest = lax.optimization_barrier(jnp.max(scores, axis=-1, keepdims=True))
    exponent_terms = jnp.exp(scores - largest)
    attn_weights = (exponent_terms / lax.optimization_barrier(jnp.sum(exponent_terms, axis=-1, keepdims=True))).astype(jnp.bfloat16)
    mixed = jnp.einsum('bkglm,bmkd->blkgd', attn_weights.astype(jnp.float32), values)
    return mixed.reshape(batch_size, length, model_width)

def project(normed, weight):
    batch_size, length, model_width = normed.shape
    flat_rows = normed.reshape(batch_size * length, model_width)
    keyval = jnp.dot(flat_rows, weight, preferred_element_type=jnp.float32).astype(jnp.bfloat16)
    return keyval.reshape(batch_size, length, weight.shape[1])

def forward_layer(rows, gain_row, weight, kv_heads, head_size):
    normed = normalize(rows.astype(jnp.float32), gain_row.astype(jnp.float32)).astype(jnp.bfloat16)
    keyval = project(normed, weight)
    mixed = attend(normed, keyval, kv_heads, head_size)
    return ((rows.astype(jnp.float32) + mixed).astype(jnp.bfloat16), keyval)

def backward_layer(rows, keyval, gain_row, weight, grad_out, kv_heads, head_size):
    batch_size, length, model_width = rows.shape
    rows_f32 = rows.astype(jnp.float32)
    normed_f32, norm_pull = jax.vjp(normalize, rows_f32, gain_row.astype(jnp.float32))
    normed = normed_f32.astype(jnp.bfloat16)
    mixed, attend_pull = jax.vjp(partial(attend, kv_heads=kv_heads, head_size=head_size), normed, keyval)
    d_normed, d_keyval = attend_pull(grad_out.astype(jnp.float32))
    flat_dkv = d_keyval.reshape(batch_size * length, weight.shape[1])
    back = lax.dot_general(flat_dkv, weight, (((1,), (1,)), ((), ())), preferred_element_type=jnp.float32)
    d_total = d_normed.astype(jnp.float32) + back.reshape(batch_size, length, model_width)
    d_rows_f32, unused_gain = norm_pull(d_total)
    inverse = lax.rsqrt(lax.optimization_barrier(jnp.mean(rows_f32 * rows_f32, axis=-1, keepdims=True)) + epsilon)
    gain_rows = d_total * (rows_f32 * inverse)
    d_rows = (grad_out.astype(jnp.float32) + d_rows_f32).astype(jnp.bfloat16)
    return (d_rows, normed, d_keyval, gain_rows)

def rounded(values):
    return lax.optimization_barrier(values.astype(jnp.bfloat16)).astype(jnp.float32)

def reference(inputs, cotangent, kv_weight, norm_gain):
    kv_cols = 2 * KVH * HD
    batch = MICRO * N_FSDP
    hidden_rows = inputs.reshape(batch, SEQ, D)
    stored_rows = []
    stored_kv = []
    for section_pos in range(SECTIONS):
        stored_rows.append(hidden_rows)
        hidden_rows, keyval = forward_layer(hidden_rows, norm_gain[section_pos], kv_weight[section_pos], KVH, HD)
        stored_kv.append(keyval)
    grad_rows = cotangent.reshape(batch, SEQ, D)
    w_list = [None] * SECTIONS
    g_list = [None] * SECTIONS
    for section_pos in range(SECTIONS - 1, -1, -1):
        grad_rows, normed, d_keyval, gain_rows = backward_layer(stored_rows[section_pos], stored_kv[section_pos], norm_gain[section_pos], kv_weight[section_pos], grad_rows, KVH, HD)
        normed_groups = normed.reshape(MICRO, N_FSDP, SEQ, D)
        dkv_groups = d_keyval.reshape(MICRO, N_FSDP, SEQ, kv_cols)
        gain_groups = gain_rows.reshape(MICRO, N_FSDP, SEQ, D)
        w_total = jnp.zeros((D, kv_cols), jnp.float32)
        g_total = jnp.zeros((D,), jnp.float32)
        for member in range(N_FSDP):
            rows_block = normed_groups[:, member].reshape(MICRO * SEQ, D)
            dkv_block = dkv_groups[:, member].reshape(MICRO * SEQ, kv_cols)
            term = lax.dot_general(rows_block, dkv_block, (((0,), (0,)), ((), ())), preferred_element_type=jnp.float32)
            w_total = w_total + rounded(term)
            g_total = g_total + rounded(lax.optimization_barrier(jnp.sum(gain_groups[:, member], axis=(0, 1))))
        w_list[section_pos] = w_total
        g_list[section_pos] = g_total
    return (jnp.stack(w_list), jnp.stack(g_list))
```

```python
from functools import partial

import jax
import jax.numpy as jnp
from jax import lax
from jax.experimental import pallas as pl
from jax.experimental.pallas import tpu as pltpu
from jax.sharding import PartitionSpec as P

HD = 128
KVH = 4
EPS = 1e-05
BLK = 128


def remote(src, dst, send_sem, recv_sem, device):
    return pltpu.make_async_remote_copy(
        src_ref=src,
        dst_ref=dst,
        send_sem=send_sem,
        recv_sem=recv_sem,
        device_id=device,
        device_id_type=pl.DeviceIdType.MESH,
    )


def nt(a, b):
    return lax.dot_general(a, b, (((1,), (1,)), ((), ())), preferred_element_type=jnp.float32)


def tn(a, b):
    return lax.dot_general(a, b, (((0,), (0,)), ((), ())), preferred_element_type=jnp.float32)


def nn(a, b):
    return jnp.dot(a, b, preferred_element_type=jnp.float32)


def kernel(
    sizes,
    in_ref, cot_ref, w_ref, gain_ref,
    out_w, out_g,
    hbuf, gbuf, wbuf, gains, nbuf, abuf, ubuf, xbuf,
    ssbuf, tbuf, rbuf,
    pbuf, r1, s1, r2, kvbuf,
    dpart, dr1, dkv, dq, gpart,
    nall, dall, gall,
    loc, a_send, a_recv, w_send, w_recv, gn_send, gn_recv,
    ss_send, ss_recv, p1_send, p1_recv, p2_send, p2_recv, p3_send, p3_recv,
    o_send, o_recv,
):
    S, F, mper, seq, df, C, D = sizes
    R = mper * F * seq
    G = F // KVH
    Rg = R // G
    H = df // HD
    NB = R // BLK
    kw = KVH * HD
    scale = HD ** (-0.5)
    me_s, me_f = lax.axis_index("section"), lax.axis_index("fsdp")
    grp, mem = lax.div(me_f, G), lax.rem(me_f, G)

    def fdev(f):
        return {"fsdp": f}

    def sdev(s):
        return {"section": s}

    barrier = pltpu.get_barrier_semaphore()
    for d in range(1, F):
        pl.semaphore_signal(barrier, inc=1, device_id=fdev(lax.rem(me_f + d, F)),
                            device_id_type=pl.DeviceIdType.MESH)
    for d in range(1, S):
        pl.semaphore_signal(barrier, inc=1, device_id=sdev(lax.rem(me_s + d, S)),
                            device_id_type=pl.DeviceIdType.MESH)
    pl.semaphore_wait(barrier, F - 1 + S - 1)

    def rows_of(m, f):
        return pl.ds(pl.multiple_of((m * F + f) * seq, seq), seq)

    def cols_of(f):
        return pl.ds(pl.multiple_of(f * df, df), df)

    def exchange_in(which, src, view):
        sends, recvs = [], []
        for m in range(mper):
            mine = me_s * mper + m
            for d in range(1, F):
                to, frm = lax.rem(me_f + d, F), lax.rem(me_f + F - d, F)
                cp = remote(src.at[mine, :, cols_of(to)], view(rows_of(m, me_f)),
                            a_send.at[which, m, d - 1], a_recv.at[which, m, d - 1], fdev(to))
                cp.start()
                sends.append(cp)
                recvs.append(remote(src.at[mine, :, cols_of(to)], view(rows_of(m, frm)),
                                    a_send.at[which, m, d - 1], a_recv.at[which, m, d - 1],
                                    fdev(to)).wait_recv)
            own = pltpu.make_async_copy(src.at[mine, :, cols_of(me_f)], view(rows_of(m, me_f)),
                                        loc.at[which, m])
            own.start()
            recvs.append(own.wait)
        return sends, recvs

    in_sends, in_recvs = exchange_in(0, in_ref, lambda rows: hbuf.at[0, rows, :])
    own_w = pltpu.make_async_copy(w_ref.at[0], wbuf.at[me_s], loc.at[2, 0])
    own_w.start()
    gains[me_s] = gain_ref[...]
    w_sends = []
    for d in range(1, S):
        to = lax.rem(me_s + d, S)
        cp = remote(gain_ref, gains.at[me_s], gn_send.at[d - 1], gn_recv.at[me_s], sdev(to))
        cp.start()
        w_sends.append(cp)
        cp = remote(w_ref.at[0], wbuf.at[me_s], w_send.at[d - 1], w_recv.at[me_s], sdev(to))
        cp.start()
        w_sends.append(cp)
    cot_sends, cot_recvs = exchange_in(1, cot_ref, lambda rows: gbuf.at[rows, :])

    for wait in in_recvs:
        wait()

    row = lax.broadcasted_iota(jnp.int32, (BLK, BLK), 0)
    col = lax.broadcasted_iota(jnp.int32, (BLK, BLK), 1)
    mask = (row >= col) & (lax.div(row, seq) == lax.div(col, seq))

    def scalars_start(buf, which, l, lanes):
        vec = jnp.sum(jnp.transpose(lanes), axis=0, keepdims=True)
        buf[l, me_f] = jnp.broadcast_to(vec, (8, R))
        for d in range(1, F):
            to = lax.rem(me_f + d, F)
            remote(buf.at[l, me_f], buf.at[l, me_f], ss_send.at[which, l, d - 1],
                   ss_recv.at[which, l, d - 1], fdev(to)).start()

    def scalars_wait(buf, which, l):
        for d in range(1, F):
            to, frm = lax.rem(me_f + d, F), lax.rem(me_f + F - d, F)
            cp = remote(buf.at[l, frm], buf.at[l, frm], ss_send.at[which, l, d - 1],
                        ss_recv.at[which, l, d - 1], fdev(to))
            cp.wait_send()
            cp.wait_recv()
        total = buf[l, 0]
        for f in range(1, F):
            total = total + buf[l, f]
        return total

    def to_column(vec8):
        return jnp.transpose(jnp.broadcast_to(vec8[:1], (HD, R)))

    my_rows = pl.ds(pl.multiple_of(mem * Rg, Rg), Rg)

    def member(j):
        return lax.rem(mem + j, G)

    def mem_rows(m):
        return pl.ds(pl.multiple_of(m * Rg, Rg), Rg)

    def to_owner(kind, l, src, dst):
        @pl.when(l != me_s)
        def _():
            remote(src, dst.at[me_s], o_send.at[kind, l], o_recv.at[kind, me_s], sdev(l)).start()

        @pl.when(l == me_s)
        def _():
            pltpu.make_async_copy(src, dst.at[me_s], o_recv.at[kind, me_s]).start()

    def forward(l, carry):
        acc = jnp.zeros((R, HD), jnp.float32)
        for hh in range(H):
            cs = slice(hh * HD, (hh + 1) * HD)
            v = hbuf[l, :, cs].astype(jnp.float32)
            acc = acc + v * v

        @pl.when(l != me_s)
        def _():
            other = lax.rem(me_s + 1, S)
            remote(gain_ref, gains.at[l], gn_send.at[0], gn_recv.at[l], sdev(other)).wait_recv()
            remote(w_ref.at[0], wbuf.at[l], w_send.at[0], w_recv.at[l], sdev(other)).wait_recv()

        @pl.when(l == me_s)
        def _():
            own_w.wait()

        scalars_start(ssbuf, 0, l, acc)
        gain = gains[l][:1]
        ubuf[...] = (hbuf[l].astype(jnp.float32) * gain).astype(jnp.bfloat16)
        for k in range(KVH):
            pbuf[l, k, :, :HD] = nn(ubuf[...], wbuf[l, :, k * HD:(k + 1) * HD]).astype(jnp.bfloat16)
            pbuf[l, k, :, HD:] = nn(
                ubuf[...], wbuf[l, :, kw + k * HD:kw + (k + 1) * HD]).astype(jnp.bfloat16)
        one = []
        for j in range(1, G):
            cp = remote(pbuf.at[l, :, mem_rows(member(j)), :], r1.at[l, j - 1],
                        p1_send.at[0, l, j - 1], p1_recv.at[0, l, j - 1],
                        fdev(grp * G + member(j)))
            cp.start()
            one.append(cp)
        total = pbuf[l, :, my_rows, :].astype(jnp.float32)
        for j in range(1, G):
            one[j - 1].wait_recv()
            total = total + r1[l, j - 1].astype(jnp.float32)
        s1[l] = total.astype(jnp.bfloat16)
        two = []
        for j in range(1, KVH):
            to = lax.rem(grp + j, KVH)
            cp = remote(s1.at[l, to], r2.at[l, j - 1], p2_send.at[0, l, j - 1],
                        p2_recv.at[0, l, j - 1], fdev(to * G + mem))
            cp.start()
            two.append(cp)
        ss = scalars_wait(ssbuf, 0, l)
        inv = to_column(lax.rsqrt(ss * (1.0 / D) + EPS))
        rbuf[l] = inv
        for hh in range(H):
            cs = slice(hh * HD, (hh + 1) * HD)
            nbuf[l, :, cs] = (
                hbuf[l, :, cs].astype(jnp.float32) * inv * gain[:, cs]).astype(jnp.bfloat16)
        to_owner(0, l, nbuf.at[l], nall)
        kv = s1[l, grp].astype(jnp.float32)
        for j in range(1, KVH):
            two[j - 1].wait_recv()
            kv = kv + r2[l, j - 1].astype(jnp.float32)
        inv_mine = rbuf[l, my_rows, :]
        kvbuf[l, my_rows, :] = jnp.concatenate(
            [kv[:, :HD] * inv_mine, kv[:, HD:] * inv_mine], axis=1).astype(jnp.bfloat16)
        three = []
        for j in range(1, G):
            cp = remote(kvbuf.at[l, my_rows, :], kvbuf.at[l, my_rows, :], p3_send.at[0, l, j - 1],
                        p3_recv.at[0, l, j - 1], fdev(grp * G + member(j)))
            cp.start()
            three.append(cp)
        for j in range(1, G):
            frm = lax.rem(mem + G - j, G)
            remote(kvbuf.at[l, mem_rows(frm), :], kvbuf.at[l, mem_rows(frm), :],
                   p3_send.at[0, l, j - 1], p3_recv.at[0, l, j - 1],
                   fdev(grp * G + member(j))).wait_recv()
        for cp in one + two + three:
            cp.wait_send()
        for b in range(NB):
            rs = slice(b * BLK, (b + 1) * BLK)
            keys, values = kvbuf[l, rs, :HD], kvbuf[l, rs, HD:]
            for hh in range(H):
                cs = slice(hh * HD, (hh + 1) * HD)
                s = jnp.where(mask, nt(nbuf[l, rs, cs], keys) * scale, -1e30)
                e = jnp.exp(s - jnp.max(s, axis=-1, keepdims=True))
                a = e / jnp.sum(e, axis=-1, keepdims=True)
                abuf[l, b * H + hh] = a
                mixed = nn(a.astype(jnp.bfloat16), values)
                hbuf[l + 1, rs, cs] = (
                    hbuf[l, rs, cs].astype(jnp.float32) + mixed).astype(jnp.bfloat16)
        return carry

    lax.fori_loop(0, S, forward, 0)

    for wait in cot_recvs:
        wait()

    def backward(step, carry):
        l = S - 1 - step
        for b in range(NB):
            rs = slice(b * BLK, (b + 1) * BLK)
            keys, values = kvbuf[l, rs, :HD], kvbuf[l, rs, HD:]
            dk = jnp.zeros((BLK, HD), jnp.float32)
            dv = jnp.zeros((BLK, HD), jnp.float32)
            acc = jnp.zeros((BLK, HD), jnp.float32)
            for hh in range(H):
                cs = slice(hh * HD, (hh + 1) * HD)
                a = abuf[l, b * H + hh]
                g = gbuf[rs, cs]
                q = nbuf[l, rs, cs]
                da = nt(g, values)
                ds = a * (da - jnp.sum(da * a, axis=-1, keepdims=True)) * scale
                ds = ds.astype(jnp.bfloat16)
                dqh = nn(ds, keys)
                dq[rs, cs] = dqh
                acc = acc + dqh * q.astype(jnp.float32)
                dk = dk + tn(ds, q)
                dv = dv + tn(a.astype(jnp.bfloat16), g)
            dpart[l, rs, :HD] = dk.astype(jnp.bfloat16)
            dpart[l, rs, HD:] = dv.astype(jnp.bfloat16)
            acc = acc + dk * keys.astype(jnp.float32) + dv * values.astype(jnp.float32)
            xbuf[rs, :] = acc
        one = []
        for j in range(1, G):
            cp = remote(dpart.at[l, mem_rows(member(j)), :], dr1.at[l, j - 1],
                        p1_send.at[1, l, j - 1], p1_recv.at[1, l, j - 1],
                        fdev(grp * G + member(j)))
            cp.start()
            one.append(cp)
        scalars_start(tbuf, 1, l, xbuf[...])
        total = dpart[l, my_rows, :].astype(jnp.float32)
        for j in range(1, G):
            one[j - 1].wait_recv()
            total = total + dr1[l, j - 1].astype(jnp.float32)
        dkv[l, grp, my_rows, :] = total.astype(jnp.bfloat16)
        two = []
        for j in range(1, KVH):
            to, frm = lax.rem(grp + j, KVH), lax.rem(grp + KVH - j, KVH)
            cp = remote(dkv.at[l, grp, my_rows, :], dkv.at[l, grp, my_rows, :],
                        p2_send.at[1, l, j - 1], p2_recv.at[1, l, j - 1], fdev(to * G + mem))
            cp.start()
            two.append(cp)
        for j in range(1, KVH):
            to, frm = lax.rem(grp + j, KVH), lax.rem(grp + KVH - j, KVH)
            remote(dkv.at[l, frm, my_rows, :], dkv.at[l, frm, my_rows, :],
                   p2_send.at[1, l, j - 1], p2_recv.at[1, l, j - 1],
                   fdev(to * G + mem)).wait_recv()
        three = []
        for j in range(1, G):
            cp = remote(dkv.at[l, :, my_rows, :], dkv.at[l, :, my_rows, :],
                        p3_send.at[1, l, j - 1], p3_recv.at[1, l, j - 1],
                        fdev(grp * G + member(j)))
            cp.start()
            three.append(cp)
        t = to_column(scalars_wait(tbuf, 1, l))
        for j in range(1, G):
            frm = lax.rem(mem + G - j, G)
            remote(dkv.at[l, :, mem_rows(frm), :], dkv.at[l, :, mem_rows(frm), :],
                   p3_send.at[1, l, j - 1], p3_recv.at[1, l, j - 1],
                   fdev(grp * G + member(j))).wait_recv()
        for cp in one + two + three:
            cp.wait_send()
        to_owner(1, l, dkv.at[l], dall)
        flat = jnp.concatenate(
            [dkv[l, k, :, :HD] for k in range(KVH)] + [dkv[l, k, :, HD:] for k in range(KVH)],
            axis=1)
        inv = rbuf[l]
        gain = gains[l][:1]
        pull = inv * inv * t * (1.0 / D)
        for hh in range(H):
            cs = slice(hh * HD, (hh + 1) * HD)
            d_total = dq[:, cs] + nt(flat, wbuf[l, cs, :])
            h = hbuf[l, :, cs].astype(jnp.float32)
            gsum = jnp.sum(d_total * (h * inv), axis=0, keepdims=True)
            gpart[l, :, cs] = jnp.broadcast_to(gsum, (8, HD))
            gbuf[:, cs] = (gbuf[:, cs].astype(jnp.float32)
                           + (d_total * (inv * gain[:, cs]) - h * pull)).astype(jnp.bfloat16)
        to_owner(2, l, gpart.at[l], gall)
        return carry

    lax.fori_loop(0, S, backward, 0)

    bufs = ((nbuf, nall), (dkv, dall), (gpart, gall))
    for kind, (src, dst) in enumerate(bufs):
        for s in range(S):
            @pl.when(s != me_s)
            def _():
                cp = remote(src.at[s], dst.at[s], o_send.at[kind, s], o_recv.at[kind, s], sdev(s))
                cp.wait_send()
                cp.wait_recv()

            @pl.when(s == me_s)
            def _():
                pltpu.make_async_copy(src.at[s], dst.at[s], o_recv.at[kind, s]).wait()
    for cp in in_sends + cot_sends + w_sends:
        cp.wait_send()

    normed = nall[...].reshape(S * R, df)
    for k in range(KVH):
        grads = tn(normed, dall[:, k].reshape(S * R, 2 * HD))
        out_w[:, k * HD:(k + 1) * HD] = grads[:, :HD]
        out_w[:, kw + k * HD:kw + (k + 1) * HD] = grads[:, HD:]
    total = gall[0]
    for s in range(1, S):
        total = total + gall[s]
    out_g[...] = total


def local(inputs, cotangent, kv_weight, norm_gain):
    S, F = lax.axis_size("section"), lax.axis_size("fsdp")
    M, seq, D = inputs.shape
    df, C = kv_weight.shape[1:]
    mper = M // S
    R = mper * F * seq
    G = F // KVH
    Rg = R // G
    H = df // HD
    gain8 = jnp.broadcast_to(norm_gain.astype(jnp.float32), (8, df))
    bf, f32 = jnp.bfloat16, jnp.float32
    V, DMA = pltpu.VMEM, pltpu.SemaphoreType.DMA
    n1 = max(G - 1, 1)
    scratch = [
        V((S + 1, R, df), bf), V((R, df), bf), V((S, df, C), bf), V((S, 8, df), f32),
        V((S, R, df), bf), V((S, R // BLK * H, BLK, BLK), f32), V((R, df), bf), V((R, HD), f32),
        V((S, F, 8, R), f32), V((S, F, 8, R), f32), V((S, R, HD), f32),
        V((S, KVH, R, 2 * HD), bf), V((S, n1, KVH, Rg, 2 * HD), bf), V((S, KVH, Rg, 2 * HD), bf),
        V((S, KVH - 1, Rg, 2 * HD), bf), V((S, R, 2 * HD), bf),
        V((S, R, 2 * HD), bf), V((S, n1, Rg, 2 * HD), bf), V((S, KVH, R, 2 * HD), bf),
        V((R, df), f32), V((S, 8, df), f32),
        V((S, R, df), bf), V((S, KVH, R, 2 * HD), bf), V((S, 8, df), f32),
        DMA((3, mper)), DMA((2, mper, F - 1)), DMA((2, mper, F - 1)),
        DMA((S - 1,)), DMA((S,)), DMA((S - 1,)), DMA((S,)),
        DMA((2, S, F - 1)), DMA((2, S, F - 1)),
        DMA((2, S, n1)), DMA((2, S, n1)), DMA((2, S, KVH - 1)), DMA((2, S, KVH - 1)),
        DMA((2, S, n1)), DMA((2, S, n1)), DMA((3, S)), DMA((3, S)),
    ]
    any_spec = pl.BlockSpec(memory_space=pl.ANY)
    vmem_spec = pl.BlockSpec(memory_space=pltpu.VMEM)
    w_share, g_share = pl.pallas_call(
        partial(kernel, (S, F, mper, seq, df, C, D)),
        out_shape=(jax.ShapeDtypeStruct((df, C), f32), jax.ShapeDtypeStruct((8, df), f32)),
        in_specs=[any_spec, any_spec, any_spec, vmem_spec],
        out_specs=(vmem_spec, vmem_spec),
        scratch_shapes=scratch,
        compiler_params=pltpu.CompilerParams(
            collective_id=0, has_side_effects=True, vmem_limit_bytes=60 * 1024 * 1024
        ),
    )(inputs, cotangent, kv_weight, gain8)
    return (w_share[None], g_share[:1])


def solution(mesh):
    in_specs = (
        P(None, "fsdp", None),
        P(None, "fsdp", None),
        P("section", "fsdp", None),
        P("section", "fsdp"),
    )
    out_specs = (P("section", "fsdp", None), P("section", "fsdp"))
    return jax.shard_map(local, mesh=mesh, in_specs=in_specs, out_specs=out_specs, check_vma=False)
```

```python
from functools import partial

import jax
import jax.numpy as jnp
from jax import lax
from jax.experimental import pallas as pl
from jax.experimental.pallas import tpu as pltpu
from jax.sharding import PartitionSpec as P

HD = 128
KVH = 4
EPS = 1e-05
BLK = 128


def remote(src, dst, send_sem, recv_sem, device):
    return pltpu.make_async_remote_copy(
        src_ref=src,
        dst_ref=dst,
        send_sem=send_sem,
        recv_sem=recv_sem,
        device_id=device,
        device_id_type=pl.DeviceIdType.MESH,
    )


def nt(a, b):
    return lax.dot_general(a, b, (((1,), (1,)), ((), ())), preferred_element_type=jnp.float32)


def tn(a, b):
    return lax.dot_general(a, b, (((0,), (0,)), ((), ())), preferred_element_type=jnp.float32)


def nn(a, b):
    return jnp.dot(a, b, preferred_element_type=jnp.float32)


def kernel(
    sizes,
    in_ref, cot_ref, w_ref, gain_ref,
    out_w, out_g,
    hbuf, gbuf, wbuf, gains, nbuf, abuf, ubuf, xbuf,
    ssbuf, tbuf, rbuf,
    pbuf, r1, s1, r2, kvbuf,
    dpart, dr1, dkv, dq, gpart,
    nall, dall, gall,
    loc, a_send, a_recv, w_send, w_recv, gn_send, gn_recv,
    ss_send, ss_recv, p1_send, p1_recv, p2_send, p2_recv, p3_send, p3_recv,
    o_send, o_recv,
):
    S, F, mper, seq, df, C, D = sizes
    R = mper * F * seq
    G = F // KVH
    Rg = R // G
    H = df // HD
    NB = R // BLK
    kw = KVH * HD
    scale = HD ** (-0.5)
    me_s, me_f = lax.axis_index("section"), lax.axis_index("fsdp")
    grp, mem = lax.div(me_f, G), lax.rem(me_f, G)

    def fdev(f):
        return {"fsdp": f}

    def sdev(s):
        return {"section": s}

    barrier = pltpu.get_barrier_semaphore()
    for d in range(1, F):
        pl.semaphore_signal(barrier, inc=1, device_id=fdev(lax.rem(me_f + d, F)),
                            device_id_type=pl.DeviceIdType.MESH)
    for d in range(1, S):
        pl.semaphore_signal(barrier, inc=1, device_id=sdev(lax.rem(me_s + d, S)),
                            device_id_type=pl.DeviceIdType.MESH)
    pl.semaphore_wait(barrier, F - 1 + S - 1)

    def rows_of(m, f):
        return pl.ds(pl.multiple_of((m * F + f) * seq, seq), seq)

    def cols_of(f):
        return pl.ds(pl.multiple_of(f * df, df), df)

    def exchange_in(which, src, view):
        sends, recvs = [], []
        for m in range(mper):
            mine = me_s * mper + m
            for d in range(1, F):
                to, frm = lax.rem(me_f + d, F), lax.rem(me_f + F - d, F)
                cp = remote(src.at[mine, :, cols_of(to)], view(rows_of(m, me_f)),
                            a_send.at[which, m, d - 1], a_recv.at[which, m, d - 1], fdev(to))
                cp.start()
                sends.append(cp)
                recvs.append(remote(src.at[mine, :, cols_of(to)], view(rows_of(m, frm)),
                                    a_send.at[which, m, d - 1], a_recv.at[which, m, d - 1],
                                    fdev(to)).wait_recv)
            own = pltpu.make_async_copy(src.at[mine, :, cols_of(me_f)], view(rows_of(m, me_f)),
                                        loc.at[which, m])
            own.start()
            recvs.append(own.wait)
        return sends, recvs

    in_sends, in_recvs = exchange_in(0, in_ref, lambda rows: hbuf.at[0, rows, :])
    own_w = pltpu.make_async_copy(w_ref.at[0], wbuf.at[me_s], loc.at[2, 0])
    own_w.start()
    gains[me_s] = gain_ref[...]
    w_sends = []
    for d in range(1, S):
        to = lax.rem(me_s + d, S)
        cp = remote(gain_ref, gains.at[me_s], gn_send.at[d - 1], gn_recv.at[me_s], sdev(to))
        cp.start()
        w_sends.append(cp)

    bits = S.bit_length() - 1
    half = df // 2

    def bit(x, i):
        return lax.rem(lax.div(x, 2 ** i), 2)

    def flip(x, i):
        return x + (1 - 2 * bit(x, i)) * 2 ** i

    def half_of(block, h):
        return wbuf.at[block, pl.ds(h * half, half), :]

    def order(h):
        return list(range(bits)) if h == 0 else list(range(bits))[::-1]

    def weight_step(step, wait):
        arriving = []
        for h in range(2):
            done, now = order(h)[:step], order(h)[step]
            for t in range(2 ** step):
                block = me_s
                for p, i in enumerate(done):
                    if (t >> p) & 1:
                        block = flip(block, i)
                to = flip(me_s, now)
                cp = remote(half_of(block, h), half_of(block, h), w_send.at[h, step, t],
                            w_recv.at[h, block], sdev(to))
                cp.start()
                w_sends.append(cp)
                came = flip(block, now)
                arriving.append(remote(half_of(came, h), half_of(came, h), w_send.at[h, step, t],
                                       w_recv.at[h, came], sdev(to)))
        if wait:
            return arriving
        return []

    own_w.wait()
    arriving = weight_step(0, bits > 1)
    cot_sends, cot_recvs = exchange_in(1, cot_ref, lambda rows: gbuf.at[rows, :])

    for wait in in_recvs:
        wait()

    for step in range(1, bits):
        for cp in arriving:
            cp.wait_recv()
        arriving = weight_step(step, step < bits - 1)

    row = lax.broadcasted_iota(jnp.int32, (BLK, BLK), 0)
    col = lax.broadcasted_iota(jnp.int32, (BLK, BLK), 1)
    mask = (row >= col) & (lax.div(row, seq) == lax.div(col, seq))

    def scalars_start(buf, which, l, lanes):
        vec = jnp.sum(jnp.transpose(lanes), axis=0, keepdims=True)
        buf[l, me_f] = jnp.broadcast_to(vec, (8, R))
        for d in range(1, F):
            to = lax.rem(me_f + d, F)
            remote(buf.at[l, me_f], buf.at[l, me_f], ss_send.at[which, l, d - 1],
                   ss_recv.at[which, l, d - 1], fdev(to)).start()

    def scalars_wait(buf, which, l):
        for d in range(1, F):
            to, frm = lax.rem(me_f + d, F), lax.rem(me_f + F - d, F)
            cp = remote(buf.at[l, frm], buf.at[l, frm], ss_send.at[which, l, d - 1],
                        ss_recv.at[which, l, d - 1], fdev(to))
            cp.wait_send()
            cp.wait_recv()
        total = buf[l, 0]
        for f in range(1, F):
            total = total + buf[l, f]
        return total

    def to_column(vec8):
        return jnp.transpose(jnp.broadcast_to(vec8[:1], (HD, R)))

    my_rows = pl.ds(pl.multiple_of(mem * Rg, Rg), Rg)

    def member(j):
        return lax.rem(mem + j, G)

    def mem_rows(m):
        return pl.ds(pl.multiple_of(m * Rg, Rg), Rg)

    def to_owner(kind, l, src, dst):
        @pl.when(l != me_s)
        def _():
            remote(src, dst.at[me_s], o_send.at[kind, l], o_recv.at[kind, me_s], sdev(l)).start()

        @pl.when(l == me_s)
        def _():
            pltpu.make_async_copy(src, dst.at[me_s], o_recv.at[kind, me_s]).start()

    def forward(l, carry):
        acc = jnp.zeros((R, HD), jnp.float32)
        for hh in range(H):
            cs = slice(hh * HD, (hh + 1) * HD)
            v = hbuf[l, :, cs].astype(jnp.float32)
            acc = acc + v * v

        @pl.when(l != me_s)
        def _():
            other = lax.rem(me_s + 1, S)
            remote(gain_ref, gains.at[l], gn_send.at[0], gn_recv.at[l], sdev(other)).wait_recv()

        for h in range(2):
            @pl.when(bit(l, order(h)[-1]) != bit(me_s, order(h)[-1]))
            def _():
                remote(half_of(l, h), half_of(l, h), w_send.at[h, 0, 0], w_recv.at[h, l],
                       sdev(flip(me_s, order(h)[-1]))).wait_recv()

        scalars_start(ssbuf, 0, l, acc)
        gain = gains[l][:1]
        ubuf[...] = (hbuf[l].astype(jnp.float32) * gain).astype(jnp.bfloat16)
        for k in range(KVH):
            pbuf[l, k, :, :HD] = nn(ubuf[...], wbuf[l, :, k * HD:(k + 1) * HD]).astype(jnp.bfloat16)
            pbuf[l, k, :, HD:] = nn(
                ubuf[...], wbuf[l, :, kw + k * HD:kw + (k + 1) * HD]).astype(jnp.bfloat16)
        one = []
        for j in range(1, G):
            cp = remote(pbuf.at[l, :, mem_rows(member(j)), :], r1.at[l, j - 1],
                        p1_send.at[0, l, j - 1], p1_recv.at[0, l, j - 1],
                        fdev(grp * G + member(j)))
            cp.start()
            one.append(cp)
        total = pbuf[l, :, my_rows, :].astype(jnp.float32)
        for j in range(1, G):
            one[j - 1].wait_recv()
            total = total + r1[l, j - 1].astype(jnp.float32)
        s1[l] = total.astype(jnp.bfloat16)
        two = []
        for j in range(1, KVH):
            to = lax.rem(grp + j, KVH)
            cp = remote(s1.at[l, to], r2.at[l, j - 1], p2_send.at[0, l, j - 1],
                        p2_recv.at[0, l, j - 1], fdev(to * G + mem))
            cp.start()
            two.append(cp)
        ss = scalars_wait(ssbuf, 0, l)
        inv = to_column(lax.rsqrt(ss * (1.0 / D) + EPS))
        rbuf[l] = inv
        for hh in range(H):
            cs = slice(hh * HD, (hh + 1) * HD)
            nbuf[l, :, cs] = (
                hbuf[l, :, cs].astype(jnp.float32) * inv * gain[:, cs]).astype(jnp.bfloat16)
        to_owner(0, l, nbuf.at[l], nall)
        kv = s1[l, grp].astype(jnp.float32)
        for j in range(1, KVH):
            two[j - 1].wait_recv()
            kv = kv + r2[l, j - 1].astype(jnp.float32)
        inv_mine = rbuf[l, my_rows, :]
        kvbuf[l, my_rows, :] = jnp.concatenate(
            [kv[:, :HD] * inv_mine, kv[:, HD:] * inv_mine], axis=1).astype(jnp.bfloat16)
        three = []
        for j in range(1, G):
            cp = remote(kvbuf.at[l, my_rows, :], kvbuf.at[l, my_rows, :], p3_send.at[0, l, j - 1],
                        p3_recv.at[0, l, j - 1], fdev(grp * G + member(j)))
            cp.start()
            three.append(cp)
        for j in range(1, G):
            frm = lax.rem(mem + G - j, G)
            remote(kvbuf.at[l, mem_rows(frm), :], kvbuf.at[l, mem_rows(frm), :],
                   p3_send.at[0, l, j - 1], p3_recv.at[0, l, j - 1],
                   fdev(grp * G + member(j))).wait_recv()
        for cp in one + two + three:
            cp.wait_send()
        for b in range(NB):
            rs = slice(b * BLK, (b + 1) * BLK)
            keys, values = kvbuf[l, rs, :HD], kvbuf[l, rs, HD:]
            for hh in range(H):
                cs = slice(hh * HD, (hh + 1) * HD)
                s = jnp.where(mask, nt(nbuf[l, rs, cs], keys) * scale, -1e30)
                e = jnp.exp(s - jnp.max(s, axis=-1, keepdims=True))
                a = e / jnp.sum(e, axis=-1, keepdims=True)
                abuf[l, b * H + hh] = a
                mixed = nn(a.astype(jnp.bfloat16), values)
                hbuf[l + 1, rs, cs] = (
                    hbuf[l, rs, cs].astype(jnp.float32) + mixed).astype(jnp.bfloat16)
        return carry

    lax.fori_loop(0, S, forward, 0)

    for wait in cot_recvs:
        wait()

    def backward(step, carry):
        l = S - 1 - step
        for b in range(NB):
            rs = slice(b * BLK, (b + 1) * BLK)
            keys, values = kvbuf[l, rs, :HD], kvbuf[l, rs, HD:]
            dk = jnp.zeros((BLK, HD), jnp.float32)
            dv = jnp.zeros((BLK, HD), jnp.float32)
            acc = jnp.zeros((BLK, HD), jnp.float32)
            for hh in range(H):
                cs = slice(hh * HD, (hh + 1) * HD)
                a = abuf[l, b * H + hh]
                g = gbuf[rs, cs]
                q = nbuf[l, rs, cs]
                da = nt(g, values)
                ds = a * (da - jnp.sum(da * a, axis=-1, keepdims=True)) * scale
                ds = ds.astype(jnp.bfloat16)
                dqh = nn(ds, keys)
                dq[rs, cs] = dqh
                acc = acc + dqh * q.astype(jnp.float32)
                dk = dk + tn(ds, q)
                dv = dv + tn(a.astype(jnp.bfloat16), g)
            dpart[l, rs, :HD] = dk.astype(jnp.bfloat16)
            dpart[l, rs, HD:] = dv.astype(jnp.bfloat16)
            acc = acc + dk * keys.astype(jnp.float32) + dv * values.astype(jnp.float32)
            xbuf[rs, :] = acc
        one = []
        for j in range(1, G):
            cp = remote(dpart.at[l, mem_rows(member(j)), :], dr1.at[l, j - 1],
                        p1_send.at[1, l, j - 1], p1_recv.at[1, l, j - 1],
                        fdev(grp * G + member(j)))
            cp.start()
            one.append(cp)
        scalars_start(tbuf, 1, l, xbuf[...])
        total = dpart[l, my_rows, :].astype(jnp.float32)
        for j in range(1, G):
            one[j - 1].wait_recv()
            total = total + dr1[l, j - 1].astype(jnp.float32)
        dkv[l, grp, my_rows, :] = total.astype(jnp.bfloat16)
        two = []
        for j in range(1, KVH):
            to, frm = lax.rem(grp + j, KVH), lax.rem(grp + KVH - j, KVH)
            cp = remote(dkv.at[l, grp, my_rows, :], dkv.at[l, grp, my_rows, :],
                        p2_send.at[1, l, j - 1], p2_recv.at[1, l, j - 1], fdev(to * G + mem))
            cp.start()
            two.append(cp)
        for j in range(1, KVH):
            to, frm = lax.rem(grp + j, KVH), lax.rem(grp + KVH - j, KVH)
            remote(dkv.at[l, frm, my_rows, :], dkv.at[l, frm, my_rows, :],
                   p2_send.at[1, l, j - 1], p2_recv.at[1, l, j - 1],
                   fdev(to * G + mem)).wait_recv()
        three = []
        for j in range(1, G):
            cp = remote(dkv.at[l, :, my_rows, :], dkv.at[l, :, my_rows, :],
                        p3_send.at[1, l, j - 1], p3_recv.at[1, l, j - 1],
                        fdev(grp * G + member(j)))
            cp.start()
            three.append(cp)
        t = to_column(scalars_wait(tbuf, 1, l))
        for j in range(1, G):
            frm = lax.rem(mem + G - j, G)
            remote(dkv.at[l, :, mem_rows(frm), :], dkv.at[l, :, mem_rows(frm), :],
                   p3_send.at[1, l, j - 1], p3_recv.at[1, l, j - 1],
                   fdev(grp * G + member(j))).wait_recv()
        for cp in one + two + three:
            cp.wait_send()
        to_owner(1, l, dkv.at[l], dall)
        flat = jnp.concatenate(
            [dkv[l, k, :, :HD] for k in range(KVH)] + [dkv[l, k, :, HD:] for k in range(KVH)],
            axis=1)
        inv = rbuf[l]
        gain = gains[l][:1]
        pull = inv * inv * t * (1.0 / D)
        for hh in range(H):
            cs = slice(hh * HD, (hh + 1) * HD)
            d_total = dq[:, cs] + nt(flat, wbuf[l, cs, :])
            h = hbuf[l, :, cs].astype(jnp.float32)
            gsum = jnp.sum(d_total * (h * inv), axis=0, keepdims=True)
            gpart[l, :, cs] = jnp.broadcast_to(gsum, (8, HD))
            gbuf[:, cs] = (gbuf[:, cs].astype(jnp.float32)
                           + (d_total * (inv * gain[:, cs]) - h * pull)).astype(jnp.bfloat16)
        to_owner(2, l, gpart.at[l], gall)
        return carry

    lax.fori_loop(0, S, backward, 0)

    bufs = ((nbuf, nall), (dkv, dall), (gpart, gall))
    for kind, (src, dst) in enumerate(bufs):
        for s in range(S):
            @pl.when(s != me_s)
            def _():
                cp = remote(src.at[s], dst.at[s], o_send.at[kind, s], o_recv.at[kind, s], sdev(s))
                cp.wait_send()
                cp.wait_recv()

            @pl.when(s == me_s)
            def _():
                pltpu.make_async_copy(src.at[s], dst.at[s], o_recv.at[kind, s]).wait()
    for cp in in_sends + cot_sends + w_sends:
        cp.wait_send()

    normed = nall[...].reshape(S * R, df)
    for k in range(KVH):
        grads = tn(normed, dall[:, k].reshape(S * R, 2 * HD))
        out_w[:, k * HD:(k + 1) * HD] = grads[:, :HD]
        out_w[:, kw + k * HD:kw + (k + 1) * HD] = grads[:, HD:]
    total = gall[0]
    for s in range(1, S):
        total = total + gall[s]
    out_g[...] = total


def local(inputs, cotangent, kv_weight, norm_gain):
    S, F = lax.axis_size("section"), lax.axis_size("fsdp")
    M, seq, D = inputs.shape
    df, C = kv_weight.shape[1:]
    mper = M // S
    R = mper * F * seq
    G = F // KVH
    Rg = R // G
    H = df // HD
    gain8 = jnp.broadcast_to(norm_gain.astype(jnp.float32), (8, df))
    bf, f32 = jnp.bfloat16, jnp.float32
    V, DMA = pltpu.VMEM, pltpu.SemaphoreType.DMA
    n1 = max(G - 1, 1)
    scratch = [
        V((S + 1, R, df), bf), V((R, df), bf), V((S, df, C), bf), V((S, 8, df), f32),
        V((S, R, df), bf), V((S, R // BLK * H, BLK, BLK), f32), V((R, df), bf), V((R, HD), f32),
        V((S, F, 8, R), f32), V((S, F, 8, R), f32), V((S, R, HD), f32),
        V((S, KVH, R, 2 * HD), bf), V((S, n1, KVH, Rg, 2 * HD), bf), V((S, KVH, Rg, 2 * HD), bf),
        V((S, KVH - 1, Rg, 2 * HD), bf), V((S, R, 2 * HD), bf),
        V((S, R, 2 * HD), bf), V((S, n1, Rg, 2 * HD), bf), V((S, KVH, R, 2 * HD), bf),
        V((R, df), f32), V((S, 8, df), f32),
        V((S, R, df), bf), V((S, KVH, R, 2 * HD), bf), V((S, 8, df), f32),
        DMA((3, mper)), DMA((2, mper, F - 1)), DMA((2, mper, F - 1)),
        DMA((2, S.bit_length() - 1, S // 2)), DMA((2, S)), DMA((S - 1,)), DMA((S,)),
        DMA((2, S, F - 1)), DMA((2, S, F - 1)),
        DMA((2, S, n1)), DMA((2, S, n1)), DMA((2, S, KVH - 1)), DMA((2, S, KVH - 1)),
        DMA((2, S, n1)), DMA((2, S, n1)), DMA((3, S)), DMA((3, S)),
    ]
    any_spec = pl.BlockSpec(memory_space=pl.ANY)
    vmem_spec = pl.BlockSpec(memory_space=pltpu.VMEM)
    w_share, g_share = pl.pallas_call(
        partial(kernel, (S, F, mper, seq, df, C, D)),
        out_shape=(jax.ShapeDtypeStruct((df, C), f32), jax.ShapeDtypeStruct((8, df), f32)),
        in_specs=[any_spec, any_spec, any_spec, vmem_spec],
        out_specs=(vmem_spec, vmem_spec),
        scratch_shapes=scratch,
        compiler_params=pltpu.CompilerParams(
            collective_id=0, has_side_effects=True, vmem_limit_bytes=60 * 1024 * 1024
        ),
    )(inputs, cotangent, kv_weight, gain8)
    return (w_share[None], g_share[:1])


def solution(mesh):
    in_specs = (
        P(None, "fsdp", None),
        P(None, "fsdp", None),
        P("section", "fsdp", None),
        P("section", "fsdp"),
    )
    out_specs = (P("section", "fsdp", None), P("section", "fsdp"))
    return jax.shard_map(local, mesh=mesh, in_specs=in_specs, out_specs=out_specs, check_vma=False)
```

```python
from functools import partial

import jax
import jax.numpy as jnp
from jax import lax
from jax.experimental import pallas as pl
from jax.experimental.pallas import tpu as pltpu
from jax.sharding import PartitionSpec as P

HD = 128
KVH = 4
EPS = 1e-05
BLK = 128


def remote(src, dst, send_sem, recv_sem, device):
    return pltpu.make_async_remote_copy(
        src_ref=src,
        dst_ref=dst,
        send_sem=send_sem,
        recv_sem=recv_sem,
        device_id=device,
        device_id_type=pl.DeviceIdType.MESH,
    )


def nt(a, b):
    return lax.dot_general(a, b, (((1,), (1,)), ((), ())), preferred_element_type=jnp.float32)


def tn(a, b):
    return lax.dot_general(a, b, (((0,), (0,)), ((), ())), preferred_element_type=jnp.float32)


def nn(a, b):
    return jnp.dot(a, b, preferred_element_type=jnp.float32)


def kernel(
    sizes,
    in_ref, cot_ref, w_ref, gain_ref,
    out_w, out_g,
    hbuf, gbuf, wbuf, gains, nbuf, abuf, ubuf, xbuf,
    ssbuf, tbuf, rbuf,
    pbuf, r1, s1, r2, kvbuf,
    dpart, dr1, dkv, dq, gpart,
    nall, dall, gall,
    loc, a_send, a_recv, w_send, w_recv, gn_send, gn_recv,
    ss_send, ss_recv, p1_send, p1_recv, p2_send, p2_recv, p3_send, p3_recv,
    o_send, o_recv,
):
    S, F, mper, seq, df, C, D = sizes
    R = mper * F * seq
    G = F // KVH
    Rg = R // G
    H = df // HD
    NB = R // BLK
    kw = KVH * HD
    scale = HD ** (-0.5)
    me_s, me_f = lax.axis_index("section"), lax.axis_index("fsdp")
    grp, mem = lax.div(me_f, G), lax.rem(me_f, G)

    def fdev(f):
        return {"fsdp": f}

    def sdev(s):
        return {"section": s}

    barrier = pltpu.get_barrier_semaphore()
    for d in range(1, F):
        pl.semaphore_signal(barrier, inc=1, device_id=fdev(lax.rem(me_f + d, F)),
                            device_id_type=pl.DeviceIdType.MESH)
    for d in range(1, S):
        pl.semaphore_signal(barrier, inc=1, device_id=sdev(lax.rem(me_s + d, S)),
                            device_id_type=pl.DeviceIdType.MESH)
    pl.semaphore_wait(barrier, F - 1 + S - 1)

    def rows_of(m, f):
        return pl.ds(pl.multiple_of((m * F + f) * seq, seq), seq)

    def cols_of(f):
        return pl.ds(pl.multiple_of(f * df, df), df)

    def exchange_in(which, src, view):
        sends, recvs = [], []
        for m in range(mper):
            mine = me_s * mper + m
            for d in range(1, F):
                to, frm = lax.rem(me_f + d, F), lax.rem(me_f + F - d, F)
                cp = remote(src.at[mine, :, cols_of(to)], view(rows_of(m, me_f)),
                            a_send.at[which, m, d - 1], a_recv.at[which, m, d - 1], fdev(to))
                cp.start()
                sends.append(cp)
                recvs.append(remote(src.at[mine, :, cols_of(to)], view(rows_of(m, frm)),
                                    a_send.at[which, m, d - 1], a_recv.at[which, m, d - 1],
                                    fdev(to)).wait_recv)
            own = pltpu.make_async_copy(src.at[mine, :, cols_of(me_f)], view(rows_of(m, me_f)),
                                        loc.at[which, m])
            own.start()
            recvs.append(own.wait)
        return sends, recvs

    in_sends, in_recvs = exchange_in(0, in_ref, lambda rows: hbuf.at[0, rows, :])
    own_w = pltpu.make_async_copy(w_ref.at[0], wbuf.at[me_s], loc.at[2, 0])
    own_w.start()
    gains[me_s] = gain_ref[...]
    w_sends = []
    for d in range(1, S):
        to = lax.rem(me_s + d, S)
        cp = remote(gain_ref, gains.at[me_s], gn_send.at[d - 1], gn_recv.at[me_s], sdev(to))
        cp.start()
        w_sends.append(cp)

    bits = S.bit_length() - 1
    half = df // 2

    def bit(x, i):
        return lax.rem(lax.div(x, 2 ** i), 2)

    def flip(x, i):
        return x + (1 - 2 * bit(x, i)) * 2 ** i

    def half_of(block, h):
        return wbuf.at[block, pl.ds(h * half, half), :]

    def order(h):
        return list(range(bits)) if h == 0 else list(range(bits))[::-1]

    def weight_step(step, wait):
        arriving = []
        for h in range(2):
            done, now = order(h)[:step], order(h)[step]
            for t in range(2 ** step):
                block = me_s
                for p, i in enumerate(done):
                    if (t >> p) & 1:
                        block = flip(block, i)
                to = flip(me_s, now)
                cp = remote(half_of(block, h), half_of(block, h), w_send.at[h, step, t],
                            w_recv.at[h, block], sdev(to))
                cp.start()
                w_sends.append(cp)
                came = flip(block, now)
                arriving.append(remote(half_of(came, h), half_of(came, h), w_send.at[h, step, t],
                                       w_recv.at[h, came], sdev(to)))
        if wait:
            return arriving
        return []

    own_w.wait()
    arriving = weight_step(0, bits > 1)

    for wait in in_recvs:
        wait()

    for step in range(1, bits):
        for cp in arriving:
            cp.wait_recv()
        arriving = weight_step(step, step < bits - 1)

    cot_sends, cot_recvs = exchange_in(1, cot_ref, lambda rows: gbuf.at[rows, :])

    row = lax.broadcasted_iota(jnp.int32, (BLK, BLK), 0)
    col = lax.broadcasted_iota(jnp.int32, (BLK, BLK), 1)
    mask = (row >= col) & (lax.div(row, seq) == lax.div(col, seq))

    def scalars_start(buf, which, l, lanes):
        vec = jnp.sum(jnp.transpose(lanes), axis=0, keepdims=True)
        buf[l, me_f] = jnp.broadcast_to(vec, (8, R))
        for d in range(1, F):
            to = lax.rem(me_f + d, F)
            remote(buf.at[l, me_f], buf.at[l, me_f], ss_send.at[which, l, d - 1],
                   ss_recv.at[which, l, d - 1], fdev(to)).start()

    def scalars_wait(buf, which, l):
        for d in range(1, F):
            to, frm = lax.rem(me_f + d, F), lax.rem(me_f + F - d, F)
            cp = remote(buf.at[l, frm], buf.at[l, frm], ss_send.at[which, l, d - 1],
                        ss_recv.at[which, l, d - 1], fdev(to))
            cp.wait_send()
            cp.wait_recv()
        total = buf[l, 0]
        for f in range(1, F):
            total = total + buf[l, f]
        return total

    def to_column(vec8):
        return jnp.transpose(jnp.broadcast_to(vec8[:1], (HD, R)))

    my_rows = pl.ds(pl.multiple_of(mem * Rg, Rg), Rg)

    def member(j):
        return lax.rem(mem + j, G)

    def mem_rows(m):
        return pl.ds(pl.multiple_of(m * Rg, Rg), Rg)

    def to_owner(kind, l, src, dst):
        @pl.when(l != me_s)
        def _():
            remote(src, dst.at[me_s], o_send.at[kind, l], o_recv.at[kind, me_s], sdev(l)).start()

        @pl.when(l == me_s)
        def _():
            pltpu.make_async_copy(src, dst.at[me_s], o_recv.at[kind, me_s]).start()

    def forward(l, carry):
        acc = jnp.zeros((R, HD), jnp.float32)
        for hh in range(H):
            cs = slice(hh * HD, (hh + 1) * HD)
            v = hbuf[l, :, cs].astype(jnp.float32)
            acc = acc + v * v

        @pl.when(l != me_s)
        def _():
            other = lax.rem(me_s + 1, S)
            remote(gain_ref, gains.at[l], gn_send.at[0], gn_recv.at[l], sdev(other)).wait_recv()

        for h in range(2):
            @pl.when(bit(l, order(h)[-1]) != bit(me_s, order(h)[-1]))
            def _():
                remote(half_of(l, h), half_of(l, h), w_send.at[h, 0, 0], w_recv.at[h, l],
                       sdev(flip(me_s, order(h)[-1]))).wait_recv()

        scalars_start(ssbuf, 0, l, acc)
        gain = gains[l][:1]
        ubuf[...] = (hbuf[l].astype(jnp.float32) * gain).astype(jnp.bfloat16)
        for k in range(KVH):
            pbuf[l, k, :, :HD] = nn(ubuf[...], wbuf[l, :, k * HD:(k + 1) * HD]).astype(jnp.bfloat16)
            pbuf[l, k, :, HD:] = nn(
                ubuf[...], wbuf[l, :, kw + k * HD:kw + (k + 1) * HD]).astype(jnp.bfloat16)
        one = []
        for j in range(1, G):
            cp = remote(pbuf.at[l, :, mem_rows(member(j)), :], r1.at[l, j - 1],
                        p1_send.at[0, l, j - 1], p1_recv.at[0, l, j - 1],
                        fdev(grp * G + member(j)))
            cp.start()
            one.append(cp)
        total = pbuf[l, :, my_rows, :].astype(jnp.float32)
        for j in range(1, G):
            one[j - 1].wait_recv()
            total = total + r1[l, j - 1].astype(jnp.float32)
        s1[l] = total.astype(jnp.bfloat16)
        two = []
        for j in range(1, KVH):
            to = lax.rem(grp + j, KVH)
            cp = remote(s1.at[l, to], r2.at[l, j - 1], p2_send.at[0, l, j - 1],
                        p2_recv.at[0, l, j - 1], fdev(to * G + mem))
            cp.start()
            two.append(cp)
        ss = scalars_wait(ssbuf, 0, l)
        inv = to_column(lax.rsqrt(ss * (1.0 / D) + EPS))
        rbuf[l] = inv
        for hh in range(H):
            cs = slice(hh * HD, (hh + 1) * HD)
            nbuf[l, :, cs] = (
                hbuf[l, :, cs].astype(jnp.float32) * inv * gain[:, cs]).astype(jnp.bfloat16)
        to_owner(0, l, nbuf.at[l], nall)
        kv = s1[l, grp].astype(jnp.float32)
        for j in range(1, KVH):
            two[j - 1].wait_recv()
            kv = kv + r2[l, j - 1].astype(jnp.float32)
        inv_mine = rbuf[l, my_rows, :]
        kvbuf[l, my_rows, :] = jnp.concatenate(
            [kv[:, :HD] * inv_mine, kv[:, HD:] * inv_mine], axis=1).astype(jnp.bfloat16)
        three = []
        for j in range(1, G):
            cp = remote(kvbuf.at[l, my_rows, :], kvbuf.at[l, my_rows, :], p3_send.at[0, l, j - 1],
                        p3_recv.at[0, l, j - 1], fdev(grp * G + member(j)))
            cp.start()
            three.append(cp)
        for j in range(1, G):
            frm = lax.rem(mem + G - j, G)
            remote(kvbuf.at[l, mem_rows(frm), :], kvbuf.at[l, mem_rows(frm), :],
                   p3_send.at[0, l, j - 1], p3_recv.at[0, l, j - 1],
                   fdev(grp * G + member(j))).wait_recv()
        for cp in one + two + three:
            cp.wait_send()
        for b in range(NB):
            rs = slice(b * BLK, (b + 1) * BLK)
            keys = kvbuf[l, rs, :HD]
            for hh in range(H):
                cs = slice(hh * HD, (hh + 1) * HD)
                s = jnp.where(mask, nt(nbuf[l, rs, cs], keys) * scale, -1e30)
                e = jnp.exp(s - jnp.max(s, axis=-1, keepdims=True))
                a = e / jnp.sum(e, axis=-1, keepdims=True)
                abuf[l, b * H + hh] = a

        @pl.when(l < S - 1)
        def _():
            for b in range(NB):
                rs = slice(b * BLK, (b + 1) * BLK)
                values = kvbuf[l, rs, HD:]
                for hh in range(H):
                    cs = slice(hh * HD, (hh + 1) * HD)
                    mixed = nn(abuf[l, b * H + hh].astype(jnp.bfloat16), values)
                    hbuf[l + 1, rs, cs] = (
                        hbuf[l, rs, cs].astype(jnp.float32) + mixed).astype(jnp.bfloat16)
        return carry

    lax.fori_loop(0, S, forward, 0)

    for wait in cot_recvs:
        wait()

    def backward(step, carry):
        l = S - 1 - step
        for b in range(NB):
            rs = slice(b * BLK, (b + 1) * BLK)
            keys, values = kvbuf[l, rs, :HD], kvbuf[l, rs, HD:]
            dk = jnp.zeros((BLK, HD), jnp.float32)
            dv = jnp.zeros((BLK, HD), jnp.float32)
            acc = jnp.zeros((BLK, HD), jnp.float32)
            for hh in range(H):
                cs = slice(hh * HD, (hh + 1) * HD)
                a = abuf[l, b * H + hh]
                g = gbuf[rs, cs]
                q = nbuf[l, rs, cs]
                da = nt(g, values)
                ds = a * (da - jnp.sum(da * a, axis=-1, keepdims=True)) * scale
                ds = ds.astype(jnp.bfloat16)
                dqh = nn(ds, keys)
                dq[rs, cs] = dqh
                acc = acc + dqh * q.astype(jnp.float32)
                dk = dk + tn(ds, q)
                dv = dv + tn(a.astype(jnp.bfloat16), g)
            dpart[l, rs, :HD] = dk.astype(jnp.bfloat16)
            dpart[l, rs, HD:] = dv.astype(jnp.bfloat16)
            acc = acc + dk * keys.astype(jnp.float32) + dv * values.astype(jnp.float32)
            xbuf[rs, :] = acc
        one = []
        for j in range(1, G):
            cp = remote(dpart.at[l, mem_rows(member(j)), :], dr1.at[l, j - 1],
                        p1_send.at[1, l, j - 1], p1_recv.at[1, l, j - 1],
                        fdev(grp * G + member(j)))
            cp.start()
            one.append(cp)
        scalars_start(tbuf, 1, l, xbuf[...])
        total = dpart[l, my_rows, :].astype(jnp.float32)
        for j in range(1, G):
            one[j - 1].wait_recv()
            total = total + dr1[l, j - 1].astype(jnp.float32)
        dkv[l, grp, my_rows, :] = total.astype(jnp.bfloat16)
        two = []
        for j in range(1, KVH):
            to, frm = lax.rem(grp + j, KVH), lax.rem(grp + KVH - j, KVH)
            cp = remote(dkv.at[l, grp, my_rows, :], dkv.at[l, grp, my_rows, :],
                        p2_send.at[1, l, j - 1], p2_recv.at[1, l, j - 1], fdev(to * G + mem))
            cp.start()
            two.append(cp)
        for j in range(1, KVH):
            to, frm = lax.rem(grp + j, KVH), lax.rem(grp + KVH - j, KVH)
            remote(dkv.at[l, frm, my_rows, :], dkv.at[l, frm, my_rows, :],
                   p2_send.at[1, l, j - 1], p2_recv.at[1, l, j - 1],
                   fdev(to * G + mem)).wait_recv()
        three = []
        for j in range(1, G):
            cp = remote(dkv.at[l, :, my_rows, :], dkv.at[l, :, my_rows, :],
                        p3_send.at[1, l, j - 1], p3_recv.at[1, l, j - 1],
                        fdev(grp * G + member(j)))
            cp.start()
            three.append(cp)
        t = to_column(scalars_wait(tbuf, 1, l))
        for j in range(1, G):
            frm = lax.rem(mem + G - j, G)
            remote(dkv.at[l, :, mem_rows(frm), :], dkv.at[l, :, mem_rows(frm), :],
                   p3_send.at[1, l, j - 1], p3_recv.at[1, l, j - 1],
                   fdev(grp * G + member(j))).wait_recv()
        for cp in one + two + three:
            cp.wait_send()
        to_owner(1, l, dkv.at[l], dall)
        flat = jnp.concatenate(
            [dkv[l, k, :, :HD] for k in range(KVH)] + [dkv[l, k, :, HD:] for k in range(KVH)],
            axis=1)
        inv = rbuf[l]
        gain = gains[l][:1]
        pull = inv * inv * t * (1.0 / D)
        for hh in range(H):
            cs = slice(hh * HD, (hh + 1) * HD)
            d_total = dq[:, cs] + nt(flat, wbuf[l, cs, :])
            h = hbuf[l, :, cs].astype(jnp.float32)
            gsum = jnp.sum(d_total * (h * inv), axis=0, keepdims=True)
            gpart[l, :, cs] = jnp.broadcast_to(gsum, (8, HD))
            gbuf[:, cs] = (gbuf[:, cs].astype(jnp.float32)
                           + (d_total * (inv * gain[:, cs]) - h * pull)).astype(jnp.bfloat16)
        to_owner(2, l, gpart.at[l], gall)
        return carry

    lax.fori_loop(0, S, backward, 0)

    bufs = ((nbuf, nall), (dkv, dall), (gpart, gall))
    for kind, (src, dst) in enumerate(bufs):
        for s in range(S):
            @pl.when(s != me_s)
            def _():
                cp = remote(src.at[s], dst.at[s], o_send.at[kind, s], o_recv.at[kind, s], sdev(s))
                cp.wait_send()
                cp.wait_recv()

            @pl.when(s == me_s)
            def _():
                pltpu.make_async_copy(src.at[s], dst.at[s], o_recv.at[kind, s]).wait()
    for cp in in_sends + cot_sends + w_sends:
        cp.wait_send()

    normed = nall[...].reshape(S * R, df)
    for k in range(KVH):
        grads = tn(normed, dall[:, k].reshape(S * R, 2 * HD))
        out_w[:, k * HD:(k + 1) * HD] = grads[:, :HD]
        out_w[:, kw + k * HD:kw + (k + 1) * HD] = grads[:, HD:]
    total = gall[0]
    for s in range(1, S):
        total = total + gall[s]
    out_g[...] = total


def local(inputs, cotangent, kv_weight, norm_gain):
    S, F = lax.axis_size("section"), lax.axis_size("fsdp")
    M, seq, D = inputs.shape
    df, C = kv_weight.shape[1:]
    mper = M // S
    R = mper * F * seq
    G = F // KVH
    Rg = R // G
    H = df // HD
    gain8 = jnp.broadcast_to(norm_gain.astype(jnp.float32), (8, df))
    bf, f32 = jnp.bfloat16, jnp.float32
    V, DMA = pltpu.VMEM, pltpu.SemaphoreType.DMA
    n1 = max(G - 1, 1)
    scratch = [
        V((S + 1, R, df), bf), V((R, df), bf), V((S, df, C), bf), V((S, 8, df), f32),
        V((S, R, df), bf), V((S, R // BLK * H, BLK, BLK), f32), V((R, df), bf), V((R, HD), f32),
        V((S, F, 8, R), f32), V((S, F, 8, R), f32), V((S, R, HD), f32),
        V((S, KVH, R, 2 * HD), bf), V((S, n1, KVH, Rg, 2 * HD), bf), V((S, KVH, Rg, 2 * HD), bf),
        V((S, KVH - 1, Rg, 2 * HD), bf), V((S, R, 2 * HD), bf),
        V((S, R, 2 * HD), bf), V((S, n1, Rg, 2 * HD), bf), V((S, KVH, R, 2 * HD), bf),
        V((R, df), f32), V((S, 8, df), f32),
        V((S, R, df), bf), V((S, KVH, R, 2 * HD), bf), V((S, 8, df), f32),
        DMA((3, mper)), DMA((2, mper, F - 1)), DMA((2, mper, F - 1)),
        DMA((2, S.bit_length() - 1, S // 2)), DMA((2, S)), DMA((S - 1,)), DMA((S,)),
        DMA((2, S, F - 1)), DMA((2, S, F - 1)),
        DMA((2, S, n1)), DMA((2, S, n1)), DMA((2, S, KVH - 1)), DMA((2, S, KVH - 1)),
        DMA((2, S, n1)), DMA((2, S, n1)), DMA((3, S)), DMA((3, S)),
    ]
    any_spec = pl.BlockSpec(memory_space=pl.ANY)
    vmem_spec = pl.BlockSpec(memory_space=pltpu.VMEM)
    w_share, g_share = pl.pallas_call(
        partial(kernel, (S, F, mper, seq, df, C, D)),
        out_shape=(jax.ShapeDtypeStruct((df, C), f32), jax.ShapeDtypeStruct((8, df), f32)),
        in_specs=[any_spec, any_spec, any_spec, vmem_spec],
        out_specs=(vmem_spec, vmem_spec),
        scratch_shapes=scratch,
        compiler_params=pltpu.CompilerParams(
            collective_id=0, has_side_effects=True, vmem_limit_bytes=60 * 1024 * 1024
        ),
    )(inputs, cotangent, kv_weight, gain8)
    return (w_share[None], g_share[:1])


def solution(mesh):
    in_specs = (
        P(None, "fsdp", None),
        P(None, "fsdp", None),
        P("section", "fsdp", None),
        P("section", "fsdp"),
    )
    out_specs = (P("section", "fsdp", None), P("section", "fsdp"))
    return jax.shard_map(local, mesh=mesh, in_specs=in_specs, out_specs=out_specs, check_vma=False)
```
